256 devices in a mesh: proc: 16 (over y, z_lo), loss: 8 (over x, z_hi), vars: 2 (over core).
Axes of the slice: x: 4, y: 4, z: 8 (z_hi: 2, z_lo: 4; z = z_hi * 4 + z_lo), core: 2. Of those that a mesh axis runs over, the one named last changes fastest.
Arguments:
- tokens: bfloat16 [32, 360, 1536], P('proc'), may hold values from -6 to 6
- shift: int32 [1], replicated, may hold values from 0 to 11
- w_qkv: bfloat16 [1536, 3, 16, 96], P(None, None, ('loss', 'vars')), may hold values from -0.15625 to 0.15625
- w_proj: bfloat16 [16, 96, 1536], replicated, may hold values from -0.15625 to 0.15625
- ln_gain: float32 [1536], replicated, may hold values from 0.1 to 1.9
- w_dec: bfloat16 [64, 4, 4, 1536], P(('loss', 'vars')), may hold values from -0.15625 to 0.15625
- prediction: bfloat16 [64, 128, 1440], P(('loss', 'vars'), 'proc'), may hold values from -6 to 6
- target: float32 [64, 128, 1440], P(('loss', 'vars'), 'proc'), may hold values from -12 to 12
- legendre: float32 [256, 128, 384], P('proc'), may hold values from -0.5 to 0.5
Outputs:
- amse: float32 [64], P(('loss', 'vars'))
- field_grad: float32 [64, 128, 1440], P(('loss', 'vars'), 'proc')
- input_grad: bfloat16 [32, 360, 1536], P('proc', None, ('loss', 'vars'))
The draws below stay inside these ranges and needn't reach their ends.
Inputs may be any that keep to these rules, and one draw needn't show every extreme that they name: `shift`: the offset is the same for all tokens.
All inputs are finite; a program needn't handle non-finite values.
Results may differ from the reference program's by a relative error of at most 0.012.
Values may be sent and summed in bfloat16 or wider, within the bound.
No kernel may reach another device: no remote copies, remote signals or barrier semaphores. Data moves between devices by JAX's collectives and lax.ppermute only.
A program may use at most 128 MiB of HBM per device.

```python
import math
import jax
import jax.numpy as jnp
from jax import lax

D = 1536
HEADS = 16
HEAD = 96
VARS = 64
LON = 1440
LDEG = 384
WR = 2
WC = 12
TC = 360
TR = 32
LAT = 128
MODES = 256


def shard_levels(own_key, dims, shards, least, largest):
    factor_of, own = 1.0, jax.random.fold_in(own_key, 6)
    for axis_at, blocks in shards:
        steps = jnp.exp(jax.random.uniform(jax.random.fold_in(own, axis_at), (blocks,), jnp.float32, least / len(shards), largest / len(shards)))
        factor_of = factor_of * jnp.repeat(steps, dims[axis_at] // blocks).reshape([-1 if axis == axis_at else 1 for axis in range(len(dims))])
    return factor_of


def gaussian(stream_key, shape, width, reach, shards=(), kind=jnp.bfloat16):
    drawn = jax.random.normal(stream_key, shape, jnp.float32) * width
    if len(shards) > 0:
        drawn = shard_levels(stream_key, shape, shards, -0.22, 0.18) * drawn
    return jnp.clip(drawn, min=-reach, max=reach).astype(kind)


def setup_inputs(seed: int = 0) -> dict:
    key_list = jax.random.split(jax.random.key(seed), 10)
    return {
        "tokens": gaussian(key_list[0], (TR, TC, D), 1.0, 6.0, ((0, 16),)),
        "shift": jax.random.randint(key_list[1], (1,), 0, WC).astype(jnp.int32),
        "w_qkv": gaussian(key_list[2], (D, 3, HEADS, HEAD), D ** -0.5, 0.15625, ((2, 16),)),
        "w_proj": gaussian(key_list[3], (HEADS, HEAD, D), D ** -0.5, 0.15625),
        "ln_gain": jnp.clip(1.0 + 0.18 * jax.random.normal(key_list[4], (D,), jnp.float32), 0.1, 1.9),
        "w_dec": gaussian(key_list[5], (VARS, 4, 4, D), D ** -0.5, 0.15625, ((0, 16),)),
        "prediction": gaussian(key_list[6], (VARS, LAT, LON), 1.0, 6.0, ((0, 16), (1, 16))),
        "target": gaussian(key_list[7], (VARS, LAT, LON), 2.0, 12.0, ((0, 16), (1, 16)), jnp.float32),
        "legendre": gaussian(key_list[8], (MODES, LAT, LDEG), LAT ** -0.5, 0.5, ((0, 16),), jnp.float32),
    }


EPSILON = 1e-06
NORM_EPSILON = 1e-05
HIGHEST = lax.Precision.HIGHEST

def fourier_basis(mode_count):
    column = jnp.arange(LON, dtype=jnp.int32)
    wavenumber = jnp.arange(mode_count, dtype=jnp.int32)
    phase = (column[:, None] * wavenumber[None, :] % LON).astype(jnp.float32) * (2.0 * math.pi / LON)
    norm_factor = 1.0 / math.sqrt(LON)
    return jnp.stack([jnp.cos(phase) * norm_factor, -jnp.sin(phase) * norm_factor])

def amse_terms(power_pred, power_true, crossed):
    amp_pred = jnp.sqrt(power_pred + EPSILON)
    amp_true = jnp.sqrt(power_true + EPSILON)
    return (amp_pred - amp_true) ** 2 + 2.0 * jnp.maximum(power_pred, power_true) * (1.0 - crossed / (amp_pred * amp_true))

def spectral_loss(field_values, target, legendre, fourier):
    fields = jnp.stack([field_values, target])
    spectra = jnp.einsum('fvao,com->fvacm', fields, fourier, precision=HIGHEST)
    harmonics = jnp.einsum('fvacm,mal->fvmcl', spectra, legendre, precision=HIGHEST)
    power_pred = lax.optimization_barrier(jnp.sum(harmonics[0] ** 2, axis=(1, 2)))
    power_true = lax.optimization_barrier(jnp.sum(harmonics[1] ** 2, axis=(1, 2)))
    crossed = lax.optimization_barrier(jnp.sum(harmonics[0] * harmonics[1], axis=(1, 2)))
    per_var = lax.optimization_barrier(jnp.sum(amse_terms(power_pred, power_true, crossed), axis=-1)) / (LDEG * MODES)
    return (jnp.mean(per_var), per_var)

def norm_parts(rolled, ln_gain):
    values = rolled.astype(jnp.float32)
    centre = lax.optimization_barrier(jnp.mean(values, axis=-1, keepdims=True))
    centred = values - centre
    variance = lax.optimization_barrier(jnp.mean(centred * centred, axis=-1, keepdims=True))
    inv_std = lax.rsqrt(variance + NORM_EPSILON)
    normed = centred * inv_std
    return (normed, inv_std, (normed * ln_gain).astype(jnp.bfloat16))

def norm_backward(grad_normed, normed, inv_std, ln_gain):
    scaled = grad_normed * ln_gain
    return inv_std * (scaled - lax.optimization_barrier(jnp.mean(scaled, axis=-1, keepdims=True)) - normed * lax.optimization_barrier(jnp.mean(scaled * normed, axis=-1, keepdims=True)))

def to_windows(values):
    row_count, col_count = (values.shape[0], values.shape[1])
    trailing = values.shape[2:]
    shaped = values.reshape((row_count // WR, WR, col_count // WC, WC) + trailing)
    shaped = jnp.moveaxis(shaped, 2, 1)
    return shaped.reshape((row_count // WR * (col_count // WC), WR * WC) + trailing)

def from_windows(values, row_count, col_count):
    trailing = values.shape[2:]
    shaped = values.reshape((row_count // WR, col_count // WC, WR, WC) + trailing)
    shaped = jnp.moveaxis(shaped, 1, 2)
    return shaped.reshape((row_count, col_count) + trailing)

def window_backward(queries, key_win, value_win, grad_out):
    score_scale = HEAD ** (-0.5)
    scores = jnp.einsum('nihe,njhe->nhij', queries.astype(jnp.float32), key_win.astype(jnp.float32)) * score_scale
    weights = jnp.exp(scores)
    weights = weights / lax.optimization_barrier(jnp.sum(weights, axis=-1, keepdims=True))
    rounded = weights.astype(jnp.bfloat16)
    grad_values = jnp.einsum('nhij,nihe->njhe', rounded.astype(jnp.float32), grad_out.astype(jnp.float32)).astype(jnp.bfloat16)
    grad_weights = jnp.einsum('nihe,njhe->nhij', grad_out.astype(jnp.float32), value_win.astype(jnp.float32))
    grad_scores = weights * (grad_weights - lax.optimization_barrier(jnp.sum(weights * grad_weights, axis=-1, keepdims=True)))
    score_round = (grad_scores * score_scale).astype(jnp.bfloat16)
    grad_queries = jnp.einsum('nhij,njhe->nihe', score_round.astype(jnp.float32), key_win.astype(jnp.float32)).astype(jnp.bfloat16)
    grad_keys = jnp.einsum('nhij,nihe->njhe', score_round.astype(jnp.float32), queries.astype(jnp.float32)).astype(jnp.bfloat16)
    return (grad_queries, grad_keys, grad_values)

def reference(tokens, shift, w_qkv, w_proj, ln_gain, w_dec, prediction, target, legendre):
    fourier = fourier_basis(MODES)
    pred_field = prediction.astype(jnp.float32)

    def total_loss(field_values):
        return spectral_loss(field_values, target, legendre, fourier)[0]
    amse = spectral_loss(pred_field, target, legendre, fourier)[1]
    field_grad = jax.grad(total_loss)(pred_field) * (LAT * LON)
    grad_round = field_grad.astype(jnp.bfloat16)
    row_count, col_count = (tokens.shape[0], tokens.shape[1])
    grad_tiles = grad_round.reshape(VARS, row_count, 4, col_count, 4)
    token_grad = jnp.einsum('vrato,vaod->rtd', grad_tiles.astype(jnp.float32), w_dec.astype(jnp.float32))
    offset = shift[0]
    rolled_grad = jnp.roll(token_grad, -offset, axis=1)
    normed, inv_std, norm_out = norm_parts(jnp.roll(tokens, -offset, axis=1), ln_gain)
    projected = jnp.einsum('rtd,dkhe->rtkhe', norm_out.astype(jnp.float32), w_qkv.astype(jnp.float32)).astype(jnp.bfloat16)
    grad_out = jnp.einsum('rtd,hed->rthe', rolled_grad, w_proj.astype(jnp.float32), precision=HIGHEST).astype(jnp.bfloat16)
    grad_queries, grad_keys, grad_values = window_backward(to_windows(projected[:, :, 0]), to_windows(projected[:, :, 1]), to_windows(projected[:, :, 2]), to_windows(grad_out))
    stacked = jnp.stack([from_windows(grad_queries, row_count, col_count), from_windows(grad_keys, row_count, col_count), from_windows(grad_values, row_count, col_count)], axis=2)
    grad_normed = jnp.einsum('rtkhe,dkhe->rtd', stacked.astype(jnp.float32), w_qkv.astype(jnp.float32))
    summed = rolled_grad + norm_backward(grad_normed, normed, inv_std, ln_gain)
    input_grad = jnp.roll(summed, offset, axis=1).astype(jnp.bfloat16)
    return (amse, field_grad, input_grad)
```

```python
import math

import jax
import jax.numpy as jnp
import ml_dtypes
import numpy as np
from jax import lax
from jax.experimental import pallas as pl
from jax.experimental.pallas import tpu as pltpu
from jax.sharding import PartitionSpec as P

HEAD = 96
VARS = 64
LAT = 128
LON = 1440
LDEG = 384
MODES = 256
D = 1536
COLS = 360
WC = 12
GROUP = 48
TOK = 2 * GROUP
PAD = 384
EPSILON = 1e-06
NORM_EPSILON = 1e-05
SCALE = HEAD ** (-0.5)
f32, bf16 = jnp.float32, jnp.bfloat16
MIB = 1 << 20


def split_table(table):
    high = table.astype(ml_dtypes.bfloat16)
    low = (table - high.astype(np.float64)).astype(ml_dtypes.bfloat16)
    return high, low


def fourier_tables():
    column, wavenumber = np.arange(LON), np.arange(MODES)
    phase = (column[:, None] * wavenumber[None, :] % LON) * (2.0 * math.pi / LON)
    basis = np.stack([np.cos(phase), -np.sin(phase)], -1) / math.sqrt(LON)
    forward = split_table(basis.reshape(LON, 2 * MODES))
    back = basis.reshape(LON, 16, 16, 2).transpose(1, 3, 2, 0).reshape(2 * MODES, LON)
    cells = np.zeros((2 * MODES, 4, PAD))
    cells[:, :, :COLS] = back.reshape(2 * MODES, COLS, 4).transpose(0, 2, 1)
    return forward, split_table(back), split_table(cells.reshape(2 * MODES, 4 * PAD))


def dot(a, b):
    return lax.dot_general(a, b, (((1,), (0,)), ((), ())), preferred_element_type=f32)


def dot_nt(a, b):
    return lax.dot_general(a, b, (((1,), (1,)), ((), ())), preferred_element_type=f32)


def halves(x):
    high = x.astype(bf16)
    return high, (x - high.astype(f32)).astype(bf16)


def row_mask(shape):
    return lax.broadcasted_iota(jnp.int32, shape, 0) < 4


def swap_rows(x):
    return pltpu.roll(x, 4, 0)


def fourier_kernel(pred_ref, targ_ref, high_ref, low_ref, out_ref):
    t_high, t_low = halves(targ_ref[...])
    rows = jnp.concatenate([pred_ref[...], t_high, t_low], axis=0)
    a = dot(rows, high_ref[...])
    b = dot(rows[:64], low_ref[...])
    y = jnp.concatenate([a[:32] + b[:32], a[32:64] + a[64:] + b[32:]], axis=0)
    for part in range(32):
        lanes = slice(part * 16, part * 16 + 16)
        out_ref[part * 8 : part * 8 + 8, :] = jnp.concatenate(
            [y[fv * 8 : fv * 8 + 8, lanes] for fv in range(8)], axis=1
        )


def split_kernel(leg_ref, high_ref, low_ref):
    for m in range(16):
        high, low = halves(leg_ref[m])
        high_ref[m] = high
        low_ref[m] = low


def legendre_kernel(spec_ref, high_ref, low_ref, harm_ref, power_ref, turned):
    power = jnp.zeros((8, LDEG), f32)
    cross = jnp.zeros((8, LDEG), f32)
    for half in range(2):
        turned[...] = spec_ref[:, half * 8 : half * 8 + 8, :].reshape(128, 128).T
        for m8 in range(8):
            m = half * 8 + m8
            rows = jnp.concatenate(
                [turned[pl.ds(m8 * 2, 8, stride=16), :], turned[pl.ds(m8 * 2 + 1, 8, stride=16), :]],
                axis=0,
            )
            r_high, r_low = halves(rows)
            both = dot(jnp.concatenate([r_high, r_low], axis=0), high_ref[m])
            h = both[:16] + both[16:] + dot(r_high, low_ref[m])
            harm_ref[m] = h
            h0, h1 = h[:8], h[8:]
            power = power + h0 * h0 + h1 * h1
            cross = cross + h0 * swap_rows(h0) + h1 * swap_rows(h1)
    first = jnp.where(row_mask((8, 128)), cross[:, :128], cross[:, 128:256])
    block = jnp.concatenate([power, first, cross[:, 256:]], axis=1)
    for q in range(16):
        power_ref[q] = block


def grad_kernel(power_ref, harm_ref, high_ref, low_ref, amse_ref, out_ref, grads):
    total = jnp.sum(power_ref[...], axis=0)
    upper = row_mask((8, LDEG))
    own = total[:, :LDEG]
    other = swap_rows(own)
    pp = jnp.where(upper, own, other)
    pt = jnp.where(upper, other, own)
    first = total[:, LDEG : LDEG + 128]
    second = swap_rows(first)
    top = row_mask((8, 128))
    cross = jnp.concatenate(
        [jnp.where(top, first, second), jnp.where(top, second, first), total[:, LDEG + 128 :]], axis=1
    )
    amp_p = jnp.sqrt(pp + EPSILON)
    amp_t = jnp.sqrt(pt + EPSILON)
    largest = jnp.maximum(pp, pt)
    incoherence = 1.0 - cross / (amp_p * amp_t)
    terms = (amp_p - amp_t) ** 2 + 2.0 * largest * incoherence
    amse = jnp.sum(terms, axis=1, keepdims=True) * (1.0 / (LDEG * MODES))
    amse_ref[...] = jnp.broadcast_to(amse, (8, 128))
    share = jnp.where(pp > pt, 1.0, jnp.where(pp == pt, 0.5, 0.0))
    grad_p = (
        (amp_p - amp_t) / amp_p
        + 2.0 * share * incoherence
        + largest * cross / (amp_p * amp_p * amp_p * amp_t)
    )
    grad_c = -2.0 * largest / (amp_p * amp_t)
    weight = LAT * LON / (VARS * LDEG * MODES)
    factor = jnp.where(upper, 2.0 * grad_p, grad_c) * weight
    for m in range(16):
        t0 = factor * harm_ref[m, 0:8, :]
        t1 = factor * harm_ref[m, 8:16, :]
        g = jnp.where(upper, t0 + swap_rows(t0), t1 + swap_rows(t1))
        high = g.astype(bf16).astype(f32)
        rows = jnp.concatenate([high, g - high], axis=0).astype(bf16)
        s = dot_nt(rows, high_ref[m]) + dot_nt(rows, low_ref[m])
        grads[m * 8 : m * 8 + 8, :] = s[:8] + s[8:]
    sorted_rows = jnp.concatenate(
        [grads[pl.ds(c * 4 + v, 16, stride=8), :] for v in range(4) for c in range(2)], axis=0
    )
    out_ref[...] = sorted_rows.T


def field_kernel(shift_ref, band_ref, high_ref, low_ref, cell_ref, field_ref, out_ref, sorted_rows):
    tiles = []
    for v in range(4):
        lanes = slice(v * 32, v * 32 + 32)
        tiles.append(jnp.concatenate([band_ref[q, :, lanes] for q in range(16)], axis=1))
    band = jnp.concatenate(tiles, axis=0)
    b_high, b_low = halves(band)
    a = dot(jnp.concatenate([b_high, b_low], axis=0), high_ref[...])
    field_ref[...] = a[:32] + a[32:] + dot(b_high, low_ref[...])
    for v in range(4):
        sorted_rows[v * 4 : v * 4 + 4, :] = tiles[v][:4]
        sorted_rows[16 + v * 4 : 20 + v * 4, :] = tiles[v][4:]
    s_high, s_low = halves(sorted_rows[...])
    g = dot(jnp.concatenate([s_high, s_low], axis=0), cell_ref[...])
    g = g[:32] + g[32:]
    g = jnp.concatenate(
        [g[r * 16 : r * 16 + 16, o * PAD : o * PAD + PAD] for r in range(2) for o in range(4)], axis=0
    )
    shift = shift_ref[0]
    column = lax.broadcasted_iota(jnp.int32, (128, PAD), 1)
    g = jnp.where(
        column < COLS - shift, pltpu.roll(g, PAD - shift, 1), pltpu.roll(g, COLS - shift, 1)
    )
    g = g.T.astype(bf16)
    for x in range(4):
        for z in range(2):
            for c in range(2):
                at = (x * 2 + c) * GROUP
                out_ref[x * 4 + z * 2 + c] = g[at : at + GROUP]


def forward_kernel(heads_ref, tok_ref, gain_ref, *refs):
    w_refs, proj_ref = refs[:8], refs[8]
    normed_ref, inv_ref, qkv_ref, values_ref, weights_ref, own_ref = refs[9:]
    x = tok_ref[...].astype(f32)
    centred = x - jnp.mean(x, axis=1, keepdims=True)
    inv = lax.rsqrt(jnp.mean(centred * centred, axis=1, keepdims=True) + NORM_EPSILON)
    normed = centred * inv
    normed_ref[...] = normed
    inv_ref[...] = jnp.broadcast_to(inv, (TOK, 128))
    norm_out = (normed * gain_ref[...]).astype(bf16)
    row_window = lax.broadcasted_iota(jnp.int32, (TOK, TOK), 0) // WC
    col_window = lax.broadcasted_iota(jnp.int32, (TOK, TOK), 1) // WC
    same = row_window % 4 == col_window % 4
    for b in range(8):
        qkv = dot_nt(w_refs[b][...], norm_out).astype(bf16)
        qkv_ref[b] = qkv
        keys = qkv[96:192].astype(f32).T.astype(bf16)
        values_ref[b] = qkv[192:].astype(f32).T.astype(bf16)
        scores = dot(keys, qkv[:96]) * SCALE
        weights = jnp.where(same, jnp.exp(scores), 0.0)
        weights_ref[b] = weights / jnp.sum(weights, axis=0, keepdims=True)
        own_ref[b * 96 : b * 96 + 96] = proj_ref[heads_ref[b]]


def backward_kernel(order_ref, flag_ref, cells_ref, gain_ref, *refs):
    w_refs, d_refs = refs[:8], refs[8:16]
    normed_ref, inv_ref, qkv_ref, values_ref, weights_ref, own_ref, out_ref = refs[16:]
    rows = [[], []]
    for p in range(8):
        near = cells_ref[order_ref[2 * p]].astype(f32)
        far = cells_ref[order_ref[2 * p + 1]].astype(f32)
        for r in range(2):
            lanes = slice(r * 64, r * 64 + 64)
            rows[r].append(jnp.concatenate([near[:, lanes], far[:, lanes]], axis=1))
    cells = jnp.concatenate([jnp.concatenate(row, axis=1) for row in rows], axis=0).astype(bf16)
    decoder = jnp.concatenate([ref[...] for ref in d_refs], axis=0)
    token_grad = dot(cells, decoder)
    t_high, t_low = halves(token_grad)
    grad_out = (dot_nt(own_ref[...], t_high) + dot_nt(own_ref[...], t_low)).astype(bf16)
    stacked = []
    for b in range(8):
        g = grad_out[b * 96 : b * 96 + 96]
        q, k = qkv_ref[b, 0:96], qkv_ref[b, 96:192]
        w = weights_ref[b]
        grad_v = dot_nt(g, w.astype(bf16))
        grad_w = dot(values_ref[b], g)
        grad_s = w * (grad_w - jnp.sum(w * grad_w, axis=0, keepdims=True))
        grad_s = (grad_s * SCALE).astype(bf16)
        stacked += [dot(k, grad_s), dot_nt(q, grad_s), grad_v]
    stacked = jnp.concatenate(stacked, axis=0).T.astype(bf16)
    weights = jnp.concatenate([ref[...] for ref in w_refs], axis=0)
    scaled = dot(stacked, weights) * gain_ref[...]
    normed = normed_ref[...]
    mean = jnp.mean(scaled, axis=1, keepdims=True)
    slope = jnp.mean(scaled * normed, axis=1, keepdims=True)
    keep = jnp.where(flag_ref[0] == 0, 1.0, 0.0)
    out = inv_ref[:, :1] * (scaled - mean - normed * slope) + keep * token_grad
    out_ref[...] = out.T.astype(bf16)


def final_kernel(shift_ref, part_ref, out_ref):
    shift = shift_ref[0]
    column = lax.broadcasted_iota(jnp.int32, (96, PAD), 1)
    sums = [
        part_ref[x * 4 + c].astype(f32) + part_ref[x * 4 + 2 + c].astype(f32)
        for x in range(4)
        for c in range(2)
    ]
    for r in range(2):
        y = jnp.concatenate([s[:, r * GROUP : r * GROUP + GROUP] for s in sums], axis=1)
        y = jnp.where(column < shift, pltpu.roll(y, shift + PAD - COLS, 1), pltpu.roll(y, shift, 1))
        out_ref[r] = y[:, :COLS].astype(bf16)


VMEM = pl.BlockSpec(memory_space=pltpu.VMEM)
SMEM = pl.BlockSpec(memory_space=pltpu.SMEM)


def call(kernel, outs, scalars, arrays, scratch=(), mib=16, flops=0, name=None):
    moved = sum(a.size * a.dtype.itemsize for a in arrays)
    moved += sum(math.prod(o.shape) * o.dtype.itemsize for o in jax.tree.leaves(outs))
    return pl.pallas_call(
        kernel,
        out_shape=outs,
        in_specs=[SMEM] * len(scalars) + [VMEM] * len(arrays),
        out_specs=jax.tree.map(lambda _: VMEM, outs),
        scratch_shapes=scratch,
        compiler_params=pltpu.CompilerParams(vmem_limit_bytes=mib * MIB),
        cost_estimate=pl.CostEstimate(flops=flops, bytes_accessed=moved, transcendentals=0),
        name=name,
    )(*scalars, *arrays)


def shape(dims, kind=f32):
    return jax.ShapeDtypeStruct(dims, kind)


def body(tokens, shift, w_qkv, w_proj, ln_gain, w_dec, prediction, target, legendre):
    forward, back, cells = fourier_tables()
    place = lax.axis_index("loss")
    x_at, z_at, core = place // 2, place % 2, lax.axis_index("vars")
    group = ("loss", "vars")
    offset = shift[0]

    def along_x(block, step):
        pairs = [(x * 2 + z, (x + step) % 4 * 2 + z) for x in range(4) for z in range(2)]
        return lax.ppermute(block, "loss", pairs)

    def along_z(block):
        return lax.ppermute(block, "loss", [(i, i ^ 1) for i in range(8)])

    def across(block):
        return lax.ppermute(block, "vars", [(0, 1), (1, 0)])

    w_own = jnp.transpose(w_qkv, (1, 2, 3, 0)).reshape(3 * HEAD, D)
    w_all = [w_own, along_x(w_own, 1), along_x(w_own, 3), along_x(w_own, 2)]
    d_own = jnp.transpose(w_dec, (2, 0, 1, 3)).reshape(64, D)
    d_own = jnp.concatenate([d_own, along_z(d_own)], axis=0)
    d_all = [d_own, along_x(d_own, 1), along_x(d_own, 3), along_x(d_own, 2)]
    w_all = w_all + [across(w) for w in w_all]
    d_all = d_all + [across(d) for d in d_all]
    places = [((x_at + dx) % 4, cc) for cc in (core, 1 - core) for dx in (0, 3, 1, 2)]
    heads = jnp.stack([(x * 2 + z_at) * 2 + c for x, c in places]).astype(jnp.int32)
    order = jnp.stack(
        [(x * 2 + z) * 2 + c for x, c in places for z in (z_at, 1 - z_at)]
    ).astype(jnp.int32)

    spectra = call(
        fourier_kernel,
        shape((256, 128)),
        [],
        [prediction.reshape(32, LON), target.reshape(32, LON), *map(jnp.asarray, forward)],
        flops=2 * 160 * LON * 512,
        name="fourier",
    ).reshape(16, 16, 128)
    at_owners = lax.all_to_all(spectra, "proc", 0, 0, tiled=True)
    leg_high, leg_low = call(
        split_kernel,
        [shape((16, LAT, LDEG), bf16), shape((16, LAT, LDEG), bf16)],
        [],
        [legendre],
        name="split",
    )
    harmonics, powers = call(
        legendre_kernel,
        [shape((16, 16, LDEG)), shape((16, 8, 640))],
        [],
        [at_owners, leg_high, leg_low],
        [pltpu.VMEM((128, 128), f32)],
        flops=2 * 48 * 16 * LAT * LDEG,
        name="legendre",
    )
    powers = lax.all_to_all(powers, "proc", 0, 0, tiled=True)
    amse, grad_spectra = call(
        grad_kernel,
        [shape((8, 128)), shape((128, 128))],
        [],
        [powers, harmonics, leg_high, leg_low],
        [pltpu.VMEM((128, 128), f32)],
        flops=2 * 32 * 16 * LAT * LDEG,
        name="grad",
    )
    banded = lax.all_to_all(grad_spectra.reshape(16, 8, 128), "proc", 0, 0, tiled=True)
    field_grad, cell_grads = call(
        field_kernel,
        [shape((32, LON)), shape((16, GROUP, 128), bf16)],
        [shift],
        [banded, *map(jnp.asarray, back), jnp.asarray(cells[0])],
        [pltpu.VMEM((32, 512), f32)],
        flops=2 * 160 * LON * 512,
        name="field",
    )
    cell_grads = lax.all_to_all(cell_grads, group, 0, 0, tiled=True)

    start = ((x_at * 2 + core) * GROUP + offset) % COLS
    wrapped = jnp.concatenate([tokens, tokens[:, :GROUP]], axis=1)
    own_tokens = lax.dynamic_slice_in_dim(wrapped, start, GROUP, 1).reshape(TOK, D)
    gain = ln_gain.reshape(1, D)
    kept = call(
        forward_kernel,
        [
            shape((TOK, D)),
            shape((TOK, 128)),
            shape((8, 3 * HEAD, TOK), bf16),
            shape((8, TOK, HEAD), bf16),
            shape((8, TOK, TOK)),
            shape((8 * HEAD, D), bf16),
        ],
        [heads],
        [own_tokens, gain, *w_all, w_proj],
        mib=40,
        flops=2 * TOK * D * 8 * 3 * HEAD,
        name="forward",
    )
    parts = call(
        backward_kernel,
        shape((D, TOK), bf16),
        [order, z_at.reshape(1).astype(jnp.int32)],
        [cell_grads, gain, *w_all, *d_all, *kept],
        mib=48,
        flops=2 * TOK * D * (8 * 3 * HEAD + 1024 + 2 * 768),
        name="backward",
    )
    parts = lax.all_to_all(parts.reshape(16, HEAD, TOK), group, 0, 0, tiled=True)
    input_grad = call(
        final_kernel, shape((2, HEAD, COLS), bf16), [shift], [parts], name="final"
    )
    return (
        amse[:4, 0],
        field_grad.reshape(4, 8, LON),
        jnp.transpose(input_grad, (0, 2, 1)),
    )


def solution(mesh):
    return jax.shard_map(
        body,
        mesh=mesh,
        in_specs=(
            P("proc", None, None),
            P(),
            P(None, None, ("loss", "vars"), None),
            P(),
            P(),
            P(("loss", "vars"), None, None, None),
            P(("loss", "vars"), "proc", None),
            P(("loss", "vars"), "proc", None),
            P("proc", None, None),
        ),
        out_specs=(
            P(("loss", "vars")),
            P(("loss", "vars"), "proc", None),
            P("proc", None, ("loss", "vars")),
        ),
        check_vma=False,
    )
```

```python
import math

import jax
import jax.numpy as jnp
import ml_dtypes
import numpy as np
from jax import lax
from jax.experimental import pallas as pl
from jax.experimental.pallas import tpu as pltpu
from jax.sharding import PartitionSpec as P

HEAD = 96
VARS = 64
LAT = 128
LON = 1440
LDEG = 384
MODES = 256
D = 1536
COLS = 360
WC = 12
GROUP = 48
TOK = 2 * GROUP
PAD = 384
EPSILON = 1e-06
NORM_EPSILON = 1e-05
SCALE = HEAD ** (-0.5)
f32, bf16 = jnp.float32, jnp.bfloat16
MIB = 1 << 20
BUSY = 1 << 33


def fourier_tables():
    column, wavenumber = np.arange(LON), np.arange(MODES)
    phase = (column[:, None] * wavenumber[None, :] % LON) * (2.0 * math.pi / LON)
    basis = np.stack([np.cos(phase), -np.sin(phase)], -1) / math.sqrt(LON)
    forward = basis.reshape(LON, 2 * MODES)
    back = basis.reshape(LON, 16, 16, 2).transpose(1, 3, 2, 0).reshape(2 * MODES, LON)
    cells = np.zeros((2 * MODES, 4, PAD))
    cells[:, :, :COLS] = back.reshape(2 * MODES, COLS, 4).transpose(0, 2, 1)
    tables = forward, back, cells.reshape(2 * MODES, 4 * PAD)
    return [jnp.asarray(table.astype(ml_dtypes.bfloat16)) for table in tables]


def dot(a, b):
    return lax.dot_general(a, b, (((1,), (0,)), ((), ())), preferred_element_type=f32)


def dot_nt(a, b):
    return lax.dot_general(a, b, (((1,), (1,)), ((), ())), preferred_element_type=f32)


def halves(x):
    high = x.astype(bf16)
    return high, (x - high.astype(f32)).astype(bf16)


def row_mask(shape):
    return lax.broadcasted_iota(jnp.int32, shape, 0) < 4


def swap_rows(x):
    return pltpu.roll(x, 4, 0)


def fetch(pairs, sems):
    copies = [pltpu.make_async_copy(src, dst, sems.at[i]) for i, (src, dst) in enumerate(pairs)]
    for copy in copies:
        copy.start()
    return copies


def fourier_kernel(pred_ref, targ_ref, table_ref, out_ref, pred, targ, table, sems):
    copies = fetch([(table_ref, table), (targ_ref, targ), (pred_ref, pred)], sems)
    for copy in copies:
        copy.wait()
    t_high, t_low = halves(targ[...])
    y = dot(jnp.concatenate([pred[...], t_high, t_low], axis=0), table[...])
    y = jnp.concatenate([y[:32], y[32:64] + y[64:]], axis=0)
    for part in range(32):
        lanes = slice(part * 16, part * 16 + 16)
        out_ref[part * 8 : part * 8 + 8, :] = jnp.concatenate(
            [y[fv * 8 : fv * 8 + 8, lanes] for fv in range(8)], axis=1
        )


def cast_kernel(leg_ref, out_ref):
    for m in range(16):
        out_ref[m] = leg_ref[m].astype(bf16)


def harmonics(spec_ref, leg_ref, turned, m):
    half, m8 = divmod(m, 8)
    if m8 == 0:
        turned[...] = spec_ref[:, half * 8 : half * 8 + 8, :].reshape(128, 128).T
    rows = [turned[pl.ds(m8 * 2 + c, 8, stride=16), :] for c in range(2)]
    high, low = halves(jnp.concatenate(rows, axis=0))
    both = dot(jnp.concatenate([high, low], axis=0), leg_ref[m])
    both = both[:16] + both[16:]
    return both[:8], both[8:]


def legendre_kernel(spec_ref, leg_ref, power_ref, turned):
    power = jnp.zeros((8, LDEG), f32)
    cross = jnp.zeros((8, LDEG), f32)
    for m in range(16):
        h0, h1 = harmonics(spec_ref, leg_ref, turned, m)
        power = power + h0 * h0 + h1 * h1
        cross = cross + h0 * swap_rows(h0) + h1 * swap_rows(h1)
    first = jnp.where(row_mask((8, 128)), cross[:, :128], cross[:, 128:256])
    block = jnp.concatenate([power, first, cross[:, 256:]], axis=1)
    for q in range(16):
        power_ref[q] = block


def grad_kernel(power_ref, spec_ref, leg_ref, amse_ref, out_ref, turned, grads, loss, sem):
    total = jnp.sum(power_ref[...], axis=0)
    upper = row_mask((8, LDEG))
    own = total[:, :LDEG]
    other = swap_rows(own)
    pp = jnp.where(upper, own, other)
    pt = jnp.where(upper, other, own)
    first = total[:, LDEG : LDEG + 128]
    second = swap_rows(first)
    top = row_mask((8, 128))
    cross = jnp.concatenate(
        [jnp.where(top, first, second), jnp.where(top, second, first), total[:, LDEG + 128 :]], axis=1
    )
    amp_p = jnp.sqrt(pp + EPSILON)
    amp_t = jnp.sqrt(pt + EPSILON)
    largest = jnp.maximum(pp, pt)
    incoherence = 1.0 - cross / (amp_p * amp_t)
    terms = (amp_p - amp_t) ** 2 + 2.0 * largest * incoherence
    amse = jnp.sum(terms, axis=1, keepdims=True) * (1.0 / (LDEG * MODES))
    loss[...] = jnp.broadcast_to(amse, (8, 128))
    copy = pltpu.make_async_copy(loss, amse_ref, sem)
    copy.start()
    share = jnp.where(pp > pt, 1.0, jnp.where(pp == pt, 0.5, 0.0))
    grad_p = (
        (amp_p - amp_t) / amp_p
        + 2.0 * share * incoherence
        + largest * cross / (amp_p * amp_p * amp_p * amp_t)
    )
    grad_c = -2.0 * largest / (amp_p * amp_t)
    weight = LAT * LON / (VARS * LDEG * MODES)
    factor = jnp.where(upper, 2.0 * grad_p, grad_c) * weight
    for m in range(16):
        h0, h1 = harmonics(spec_ref, leg_ref, turned, m)
        t0, t1 = factor * h0, factor * h1
        g = jnp.where(upper, t0 + swap_rows(t0), t1 + swap_rows(t1))
        high = g.astype(bf16).astype(f32)
        s = dot_nt(jnp.concatenate([high, g - high], axis=0).astype(bf16), leg_ref[m])
        grads[m * 8 : m * 8 + 8, :] = s[:8] + s[8:]
    sorted_rows = jnp.concatenate(
        [grads[pl.ds(c * 4 + v, 16, stride=8), :] for v in range(4) for c in range(2)], axis=0
    )
    out_ref[...] = sorted_rows.T
    copy.wait()


def pair_kernel(own_ref, far_ref, out_ref):
    size = own_ref.shape[0]
    out_ref[:size] = own_ref[...]
    out_ref[size:] = far_ref[...]


def table_kernel(tick_ref, table_ref, cell_ref, table, cell, sems):
    for copy in fetch([(cell_ref, cell), (table_ref, table)], sems):
        copy.wait()


def field_kernel(shift_ref, band_ref, table, cell, field_ref, out_ref, field, sorted_rows, sem):
    tiles = []
    for v in range(4):
        lanes = slice(v * 32, v * 32 + 32)
        tiles.append(jnp.concatenate([band_ref[q, :, lanes] for q in range(16)], axis=1))
    for v in range(4):
        sorted_rows[v * 4 : v * 4 + 4, :] = tiles[v][:4]
        sorted_rows[16 + v * 4 : 20 + v * 4, :] = tiles[v][4:]
    b_high, b_low = halves(jnp.concatenate(tiles, axis=0))
    a = dot(jnp.concatenate([b_high, b_low], axis=0), table[...])
    field[...] = a[:32] + a[32:]
    store = pltpu.make_async_copy(field, field_ref, sem)
    store.start()
    s_high, s_low = halves(sorted_rows[...])
    g = dot(jnp.concatenate([s_high, s_low], axis=0), cell[...])
    g = g[:32] + g[32:]
    g = jnp.concatenate(
        [g[r * 16 : r * 16 + 16, o * PAD : o * PAD + PAD] for r in range(2) for o in range(4)], axis=0
    )
    shift = shift_ref[0]
    column = lax.broadcasted_iota(jnp.int32, (128, PAD), 1)
    g = jnp.where(
        column < COLS - shift, pltpu.roll(g, PAD - shift, 1), pltpu.roll(g, COLS - shift, 1)
    )
    g = g.T.astype(bf16)
    for x in range(4):
        for z in range(2):
            for c in range(2):
                at = (x * 2 + c) * GROUP
                out_ref[x * 4 + z * 2 + c] = g[at : at + GROUP]
    store.wait()


def norm_rows(tok_ref, gain_ref):
    x = tok_ref[...].astype(f32)
    centred = x - jnp.mean(x, axis=1, keepdims=True)
    inv = lax.rsqrt(jnp.mean(centred * centred, axis=1, keepdims=True) + NORM_EPSILON)
    return centred * inv, inv


def attention_kernel(gain_ref, cells_ref, tok_ref, proj_ref, *refs):
    w_refs, d_refs, out_ref = refs[:8], refs[8:12], refs[12]
    got, tok, decoder, proj, w, sems = refs[13:]
    place, core = lax.axis_index("loss"), lax.axis_index("vars")
    x_at, z_at = place // 2, place % 2
    places = [((x_at + dx) % 4, c) for c in (core, 1 - core) for dx in (0, 3, 1, 2)]
    first = fetch([(tok_ref, tok), (cells_ref, got)], sems.at[0])
    w_copies = [
        pltpu.make_async_copy(w_refs[b], w.at[pl.ds(b * 288, 288)], sems.at[1, b]) for b in range(8)
    ]
    for copy in w_copies[:4]:
        copy.start()
    gain = gain_ref[...]
    row_window = lax.broadcasted_iota(jnp.int32, (TOK, TOK), 0) // WC
    col_window = lax.broadcasted_iota(jnp.int32, (TOK, TOK), 1) // WC
    same = row_window % 4 == col_window % 4
    first[0].wait()
    x = tok[...].astype(f32)
    centred = x - jnp.mean(x, axis=1, keepdims=True)
    inv = lax.rsqrt(jnp.mean(centred * centred, axis=1, keepdims=True) + NORM_EPSILON)
    normed = centred * inv
    norm_out = (normed * gain).astype(bf16)
    heads = []
    for b in range(8):
        if b % 2 == 0:
            for i in (b, b + 1):
                w_copies[i].wait()
                if i < 4:
                    w_copies[i + 4].start()
            both = dot_nt(w[b * 288 : b * 288 + 576], norm_out).astype(bf16)
        if b == 4:
            d_copies = fetch(
                [(d_refs[i], decoder.at[pl.ds(i * 256, 256)]) for i in range(4)], sems.at[2]
            )
            p_copies = fetch(
                [
                    (proj_ref.at[(x * 2 + z_at) * 2 + c], proj.at[pl.ds(i * 96, 96)])
                    for i, (x, c) in enumerate(places)
                ],
                sems.at[3],
            )
        at = b % 2 * 288
        q, k, v = [both[at + i * 96 : at + i * 96 + 96] for i in range(3)]
        keys = k.astype(f32).T.astype(bf16)
        values = v.astype(f32).T.astype(bf16)
        a = jnp.where(same, jnp.exp(dot(keys, q) * SCALE), 0.0)
        heads.append((q, k, values, a / jnp.sum(a, axis=0, keepdims=True)))
    first[1].wait()
    rows = [[], []]
    for x_from, c_from in [(x_at ^ k, c) for c in (core, 1 - core) for k in range(4)]:
        near = got[(x_from * 2 + z_at) * 2 + c_from].astype(f32)
        far = got[(x_from * 2 + 1 - z_at) * 2 + c_from].astype(f32)
        for r in range(2):
            lanes = slice(r * 64, r * 64 + 64)
            rows[r].append(jnp.concatenate([near[:, lanes], far[:, lanes]], axis=1))
    cells = jnp.concatenate([jnp.concatenate(row, axis=1) for row in rows], axis=0).astype(bf16)
    for copy in d_copies:
        copy.wait()
    token_grad = dot(cells, decoder[...])
    for copy in p_copies:
        copy.wait()
    grad_out = dot_nt(proj[...], token_grad.astype(bf16)).astype(bf16)
    stacked = []
    for b in range(8):
        q, k, values, a = heads[b]
        g = grad_out[b * 96 : b * 96 + 96]
        grad_v = dot_nt(g, a.astype(bf16))
        grad_a = dot(values, g)
        grad_s = a * (grad_a - jnp.sum(a * grad_a, axis=0, keepdims=True))
        grad_s = (grad_s * SCALE).astype(bf16)
        stacked += [dot(k, grad_s), dot_nt(q, grad_s), grad_v]
    stacked = jnp.concatenate(stacked, axis=0).T.astype(bf16)
    scaled = dot(stacked, w[...]) * gain
    mean = jnp.mean(scaled, axis=1, keepdims=True)
    slope = jnp.mean(scaled * normed, axis=1, keepdims=True)
    keep = jnp.where(z_at == 0, 1.0, 0.0)
    out = inv * (scaled - mean - normed * slope) + keep * token_grad
    out = out.T
    packed = []
    for g in range(16):
        tail = out[g * 96 + 72 : g * 96 + 96]
        for part in range(3):
            body = out[g * 96 + part * 24 : g * 96 + part * 24 + 24]
            packed.append(jnp.concatenate([body, tail[:, part * 32 : part * 32 + 32]], axis=1))
    out_ref[...] = jnp.concatenate(packed, axis=0).astype(bf16)


def final_kernel(shift_ref, part_ref, out_ref):
    shift = shift_ref[0]
    column = lax.broadcasted_iota(jnp.int32, (96, PAD), 1)
    parts = part_ref[...].astype(f32)
    sums = []
    for x in range(4):
        for c in range(2):
            at = (x * 4 + c) * 72
            s = parts[at : at + 72] + parts[at + 144 : at + 216]
            tail = jnp.concatenate([s[i * 24 : i * 24 + 24, 96:] for i in range(3)], axis=1)
            sums.append(jnp.concatenate([s[:, :96], tail], axis=0))
    for r in range(2):
        y = jnp.concatenate([s[:, r * GROUP : r * GROUP + GROUP] for s in sums], axis=1)
        y = jnp.where(column < shift, pltpu.roll(y, shift + PAD - COLS, 1), pltpu.roll(y, shift, 1))
        out_ref[r] = y[:, :COLS].astype(bf16)


VMEM = pl.BlockSpec(memory_space=pltpu.VMEM)
SMEM = pl.BlockSpec(memory_space=pltpu.SMEM)
HBM = pl.BlockSpec(memory_space=pltpu.HBM)


def call(kernel, outs, scalars, near, far=(), scratch=(), mib=16, flops=0, name=None, spaces=VMEM):
    arrays = [*near, *far]
    moved = sum(a.size * a.dtype.itemsize for a in arrays)
    moved += sum(math.prod(o.shape) * o.dtype.itemsize for o in jax.tree.leaves(outs))
    if isinstance(outs, list) and not isinstance(spaces, list):
        spaces = [spaces] * len(outs)
    return pl.pallas_call(
        kernel,
        out_shape=outs,
        in_specs=[SMEM] * len(scalars) + [VMEM] * len(near) + [HBM] * len(far),
        out_specs=spaces,
        scratch_shapes=scratch,
        compiler_params=pltpu.CompilerParams(vmem_limit_bytes=mib * MIB),
        cost_estimate=pl.CostEstimate(flops=flops, bytes_accessed=moved, transcendentals=0),
        name=name,
    )(*scalars, *arrays)


def shape(dims, kind=f32):
    return jax.ShapeDtypeStruct(dims, kind)


def body(tokens, shift, w_qkv, w_proj, ln_gain, w_dec, prediction, target, legendre):
    forward, back, cells = fourier_tables()
    place = lax.axis_index("loss")
    x_at, z_at, core = place // 2, place % 2, lax.axis_index("vars")
    group = ("loss", "vars")
    offset = shift[0]

    def along_x(block, step):
        pairs = [(x * 2 + z, (x + step) % 4 * 2 + z) for x in range(4) for z in range(2)]
        return lax.ppermute(block, "loss", pairs)

    def along_z(block):
        return lax.ppermute(block, "loss", [(i, i ^ 1) for i in range(8)])

    def across(block):
        return lax.ppermute(block, "vars", [(0, 1), (1, 0)])

    def after(block, earlier):
        return lax.optimization_barrier((block, earlier))[0]

    w_own = jnp.transpose(w_qkv, (1, 2, 3, 0)).reshape(3 * HEAD, D)
    w_all = [w_own, along_x(w_own, 1), along_x(w_own, 3), along_x(w_own, 2)]
    spectra = call(
        fourier_kernel,
        shape((256, 128)),
        [],
        [],
        [prediction.reshape(32, LON), target.reshape(32, LON), forward],
        scratch=[
            pltpu.VMEM((32, LON), bf16),
            pltpu.VMEM((32, LON), f32),
            pltpu.VMEM((LON, 512), bf16),
            pltpu.SemaphoreType.DMA((3,)),
        ],
        mib=60,
        flops=2 * 160 * LON * 512,
        name="fourier",
    )
    at_owners = lax.all_to_all(spectra.reshape(16, 16, 128), "proc", 0, 0, tiled=True)
    leg = call(
        cast_kernel,
        shape((16, LAT, LDEG), bf16),
        [],
        [after(legendre, spectra)],
        flops=BUSY,
        name="cast",
    )
    d_own = jnp.transpose(w_dec, (2, 0, 1, 3)).reshape(64, D)
    d_far = along_z(after(d_own, leg))
    w_all.append(across(after(w_own, leg)))
    powers = call(
        legendre_kernel,
        shape((16, 8, 640)),
        [],
        [at_owners, leg],
        scratch=[pltpu.VMEM((128, 128), f32)],
        flops=2 * 48 * 16 * LAT * LDEG,
        name="legendre",
    )
    d_own = call(
        pair_kernel,
        shape((128, D), bf16),
        [],
        [*after((d_own, d_far), (powers, w_all[4]))],
        flops=BUSY,
        name="pair",
    )
    d_far = lax.ppermute(d_own, "loss", [(i, i ^ 2) for i in range(8)])
    powers = lax.all_to_all(powers, "proc", 0, 0, tiled=True)
    amse, grad_spectra = call(
        grad_kernel,
        [shape((8, 128)), shape((128, 128))],
        [],
        [after(powers, d_own), at_owners, leg],
        scratch=[
            pltpu.VMEM((128, 128), f32),
            pltpu.VMEM((128, 128), f32),
            pltpu.VMEM((8, 128), f32),
            pltpu.SemaphoreType.DMA,
        ],
        flops=2 * 80 * 16 * LAT * LDEG,
        name="grad",
        spaces=[HBM, VMEM],
    )
    banded = lax.all_to_all(grad_spectra.reshape(16, 8, 128), "proc", 0, 0, tiled=True)
    start = ((x_at * 2 + core) * GROUP + offset) % COLS
    back, cells = call(
        table_kernel,
        [shape((512, LON), bf16), shape((512, 4 * PAD), bf16)],
        [],
        [],
        [after(grad_spectra, w_all[1:3]), back, cells],
        scratch=[pltpu.SemaphoreType.DMA((2,))],
        flops=BUSY,
        name="tables",
    )
    w_all += [across(after(w, back)) for w in w_all[1:3]]
    d_own = call(
        pair_kernel,
        shape((256, D), bf16),
        [],
        [*after((d_own, d_far), grad_spectra)],
        flops=BUSY,
        name="pair2",
    )
    d_far = along_x(d_own, 2)
    d_all = [d_own, d_far, across(after(d_own, back))]
    field_grad, cell_grads = call(
        field_kernel,
        [shape((32, LON)), shape((16, GROUP, 128), bf16)],
        [shift],
        [banded, back, cells],
        scratch=[
            pltpu.VMEM((32, LON), f32),
            pltpu.VMEM((32, 512), f32),
            pltpu.SemaphoreType.DMA,
        ],
        flops=2 * 160 * LON * 512,
        name="field",
        spaces=[HBM, VMEM],
    )
    w_all.append(across(after(w_all[3], cell_grads)))
    own_tokens = after(tokens, cell_grads)
    own_tokens = jnp.concatenate([own_tokens, own_tokens[:, :GROUP]], axis=1)
    own_tokens = lax.dynamic_slice_in_dim(own_tokens, start, GROUP, 1).reshape(TOK, D)
    cell_grads = lax.all_to_all(cell_grads, group, 0, 0, tiled=True)
    d_all.append(across(after(d_far, cell_grads)))
    parts = call(
        attention_kernel,
        shape((16 * 72, 128), bf16),
        [],
        [ln_gain.reshape(1, D)],
        [cell_grads, own_tokens, w_proj, *w_all, *d_all],
        scratch=[
            pltpu.VMEM((16, GROUP, 128), bf16),
            pltpu.VMEM((TOK, D), bf16),
            pltpu.VMEM((1024, D), bf16),
            pltpu.VMEM((8 * HEAD, D), bf16),
            pltpu.VMEM((8 * 3 * HEAD, D), bf16),
            pltpu.SemaphoreType.DMA((4, 8)),
        ],
        mib=60,
        flops=2 * TOK * D * (16 * 3 * HEAD + 1024 + 768),
        name="attention",
    )
    parts = lax.all_to_all(parts.reshape(16, 72, 128), group, 0, 0, tiled=True)
    input_grad = call(
        final_kernel, shape((2, HEAD, COLS), bf16), [shift], [parts.reshape(16 * 72, 128)], name="final"
    )
    return (
        amse[:4, 0],
        field_grad.reshape(4, 8, LON),
        jnp.transpose(input_grad, (0, 2, 1)),
    )


def solution(mesh):
    return jax.shard_map(
        body,
        mesh=mesh,
        in_specs=(
            P("proc", None, None),
            P(),
            P(None, None, ("loss", "vars"), None),
            P(),
            P(),
            P(("loss", "vars"), None, None, None),
            P(("loss", "vars"), "proc", None),
            P(("loss", "vars"), "proc", None),
            P("proc", None, None),
        ),
        out_specs=(
            P(("loss", "vars")),
            P(("loss", "vars"), "proc", None),
            P("proc", None, ("loss", "vars")),
        ),
        check_vma=False,
    )
```

```python
import math

import jax
import jax.numpy as jnp
import ml_dtypes
import numpy as np
from jax import lax
from jax.experimental import pallas as pl
from jax.experimental.pallas import tpu as pltpu
from jax.sharding import PartitionSpec as P

HEAD = 96
VARS = 64
LAT = 128
LON = 1440
LDEG = 384
MODES = 256
D = 1536
COLS = 360
WC = 12
GROUP = 48
TOK = 2 * GROUP
PAD = 384
EPSILON = 1e-06
NORM_EPSILON = 1e-05
SCALE = HEAD ** (-0.5)
f32, bf16 = jnp.float32, jnp.bfloat16
MIB = 1 << 20
BUSY = 1 << 33


def fourier_tables():
    column, wavenumber = np.arange(LON), np.arange(MODES)
    phase = (column[:, None] * wavenumber[None, :] % LON) * (2.0 * math.pi / LON)
    basis = np.stack([np.cos(phase), -np.sin(phase)], -1) / math.sqrt(LON)
    forward = basis.reshape(LON, 2 * MODES)
    back = basis.reshape(LON, 16, 16, 2).transpose(1, 3, 2, 0).reshape(2 * MODES, LON)
    cells = np.zeros((2 * MODES, 4, PAD))
    cells[:, :, :COLS] = back.reshape(2 * MODES, COLS, 4).transpose(0, 2, 1)
    tables = forward, back, cells.reshape(2 * MODES, 4 * PAD)
    return [jnp.asarray(table.astype(ml_dtypes.bfloat16)) for table in tables]


def dot(a, b):
    return lax.dot_general(a, b, (((1,), (0,)), ((), ())), preferred_element_type=f32)


def dot_nt(a, b):
    return lax.dot_general(a, b, (((1,), (1,)), ((), ())), preferred_element_type=f32)


def halves(x):
    high = x.astype(bf16)
    return high, (x - high.astype(f32)).astype(bf16)


def row_mask(shape):
    return lax.broadcasted_iota(jnp.int32, shape, 0) < 4


def swap_rows(x):
    return pltpu.roll(x, 4, 0)


def fetch(pairs, sems):
    copies = [pltpu.make_async_copy(src, dst, sems.at[i]) for i, (src, dst) in enumerate(pairs)]
    for copy in copies:
        copy.start()
    return copies


def fourier_kernel(pred_ref, targ_ref, table_ref, out_ref, pred, targ, table, sems):
    copies = fetch([(table_ref, table), (targ_ref, targ), (pred_ref, pred)], sems)
    for copy in copies:
        copy.wait()
    t_high, t_low = halves(targ[...])
    y = dot(jnp.concatenate([pred[...], t_high, t_low], axis=0), table[...])
    y = jnp.concatenate([y[:32], y[32:64] + y[64:]], axis=0)
    for part in range(32):
        lanes = slice(part * 16, part * 16 + 16)
        out_ref[part * 8 : part * 8 + 8, :] = jnp.concatenate(
            [y[fv * 8 : fv * 8 + 8, lanes] for fv in range(8)], axis=1
        )


def cast_kernel(leg_ref, out_ref):
    for m in range(16):
        out_ref[m] = leg_ref[m].astype(bf16)


def harmonics(spec_ref, leg_ref, turned, m):
    half, m8 = divmod(m, 8)
    if m8 == 0:
        turned[...] = spec_ref[:, half * 8 : half * 8 + 8, :].reshape(128, 128).T
    rows = [turned[pl.ds(m8 * 2 + c, 8, stride=16), :] for c in range(2)]
    high, low = halves(jnp.concatenate(rows, axis=0))
    both = dot(jnp.concatenate([high, low], axis=0), leg_ref[m])
    both = both[:16] + both[16:]
    return both[:8], both[8:]


def legendre_kernel(spec_ref, leg_ref, power_ref, turned):
    power = jnp.zeros((8, LDEG), f32)
    cross = jnp.zeros((8, LDEG), f32)
    for m in range(16):
        h0, h1 = harmonics(spec_ref, leg_ref, turned, m)
        power = power + h0 * h0 + h1 * h1
        cross = cross + h0 * swap_rows(h0) + h1 * swap_rows(h1)
    first = jnp.where(row_mask((8, 128)), cross[:, :128], cross[:, 128:256])
    block = jnp.concatenate([power, first, cross[:, 256:]], axis=1)
    for q in range(16):
        power_ref[q] = block


def grad_kernel(power_ref, spec_ref, leg_ref, amse_ref, out_ref, turned, grads, loss, sem):
    total = jnp.sum(power_ref[...], axis=0)
    upper = row_mask((8, LDEG))
    own = total[:, :LDEG]
    other = swap_rows(own)
    pp = jnp.where(upper, own, other)
    pt = jnp.where(upper, other, own)
    first = total[:, LDEG : LDEG + 128]
    second = swap_rows(first)
    top = row_mask((8, 128))
    cross = jnp.concatenate(
        [jnp.where(top, first, second), jnp.where(top, second, first), total[:, LDEG + 128 :]], axis=1
    )
    amp_p = jnp.sqrt(pp + EPSILON)
    amp_t = jnp.sqrt(pt + EPSILON)
    largest = jnp.maximum(pp, pt)
    incoherence = 1.0 - cross / (amp_p * amp_t)
    terms = (amp_p - amp_t) ** 2 + 2.0 * largest * incoherence
    amse = jnp.sum(terms, axis=1, keepdims=True) * (1.0 / (LDEG * MODES))
    loss[...] = jnp.broadcast_to(amse, (8, 128))
    copy = pltpu.make_async_copy(loss, amse_ref, sem)
    copy.start()
    share = jnp.where(pp > pt, 1.0, jnp.where(pp == pt, 0.5, 0.0))
    grad_p = (
        (amp_p - amp_t) / amp_p
        + 2.0 * share * incoherence
        + largest * cross / (amp_p * amp_p * amp_p * amp_t)
    )
    grad_c = -2.0 * largest / (amp_p * amp_t)
    weight = LAT * LON / (VARS * LDEG * MODES)
    factor = jnp.where(upper, 2.0 * grad_p, grad_c) * weight
    for m in range(16):
        h0, h1 = harmonics(spec_ref, leg_ref, turned, m)
        t0, t1 = factor * h0, factor * h1
        g = jnp.where(upper, t0 + swap_rows(t0), t1 + swap_rows(t1))
        high = g.astype(bf16).astype(f32)
        s = dot_nt(jnp.concatenate([high, g - high], axis=0).astype(bf16), leg_ref[m])
        grads[m * 8 : m * 8 + 8, :] = s[:8] + s[8:]
    sorted_rows = jnp.concatenate(
        [grads[pl.ds(c * 4 + v, 16, stride=8), :] for v in range(4) for c in range(2)], axis=0
    )
    out_ref[...] = sorted_rows.T
    copy.wait()


def pair_kernel(own_ref, far_ref, out_ref):
    size = own_ref.shape[0]
    out_ref[:size] = own_ref[...]
    out_ref[size:] = far_ref[...]


def table_kernel(tick_ref, table_ref, cell_ref, table, cell, sems):
    for copy in fetch([(cell_ref, cell), (table_ref, table)], sems):
        copy.wait()


def field_kernel(shift_ref, band_ref, table, cell, field_ref, out_ref, field, sorted_rows, sem):
    tiles = []
    for v in range(4):
        lanes = slice(v * 32, v * 32 + 32)
        tiles.append(jnp.concatenate([band_ref[q, :, lanes] for q in range(16)], axis=1))
    for v in range(4):
        sorted_rows[v * 4 : v * 4 + 4, :] = tiles[v][:4]
        sorted_rows[16 + v * 4 : 20 + v * 4, :] = tiles[v][4:]
    b_high, b_low = halves(jnp.concatenate(tiles, axis=0))
    a = dot(jnp.concatenate([b_high, b_low], axis=0), table[...])
    field[...] = a[:32] + a[32:]
    store = pltpu.make_async_copy(field, field_ref, sem)
    store.start()
    s_high, s_low = halves(sorted_rows[...])
    g = dot(jnp.concatenate([s_high, s_low], axis=0), cell[...])
    g = g[:32] + g[32:]
    g = jnp.concatenate(
        [g[r * 16 : r * 16 + 16, o * PAD : o * PAD + PAD] for r in range(2) for o in range(4)], axis=0
    )
    shift = shift_ref[0]
    column = lax.broadcasted_iota(jnp.int32, (128, PAD), 1)
    g = jnp.where(
        column < COLS - shift, pltpu.roll(g, PAD - shift, 1), pltpu.roll(g, COLS - shift, 1)
    )
    g = g.T.astype(bf16)
    for x in range(4):
        for z in range(2):
            for c in range(2):
                at = (x * 2 + c) * GROUP
                out_ref[x * 4 + z * 2 + c] = g[at : at + GROUP]
    store.wait()


def norm_rows(tok_ref, gain_ref):
    x = tok_ref[...].astype(f32)
    centred = x - jnp.mean(x, axis=1, keepdims=True)
    inv = lax.rsqrt(jnp.mean(centred * centred, axis=1, keepdims=True) + NORM_EPSILON)
    return centred * inv, inv


def attention_kernel(gain_ref, cells_ref, tok_ref, proj_ref, *refs):
    w_refs, d_refs, out_ref = refs[:8], refs[8:12], refs[12]
    got, tok, decoder, proj, w, sems = refs[13:]
    place, core = lax.axis_index("loss"), lax.axis_index("vars")
    x_at, z_at = place // 2, place % 2
    places = [((x_at + dx) % 4, c) for c in (core, 1 - core) for dx in (0, 3, 1, 2)]
    first = fetch([(tok_ref, tok), (cells_ref, got)], sems.at[0])
    w_copies = [
        pltpu.make_async_copy(w_refs[b], w.at[pl.ds(b * 288, 288)], sems.at[1, b]) for b in range(8)
    ]
    for copy in w_copies[:4]:
        copy.start()
    gain = gain_ref[...]
    row_window = lax.broadcasted_iota(jnp.int32, (TOK, TOK), 0) // WC
    col_window = lax.broadcasted_iota(jnp.int32, (TOK, TOK), 1) // WC
    same = row_window % 4 == col_window % 4
    first[0].wait()
    x = tok[...].astype(f32)
    centred = x - jnp.mean(x, axis=1, keepdims=True)
    inv = lax.rsqrt(jnp.mean(centred * centred, axis=1, keepdims=True) + NORM_EPSILON)
    normed = centred * inv
    norm_out = (normed * gain).astype(bf16)
    heads = []
    for b in range(8):
        if b % 2 == 0:
            for i in (b, b + 1):
                w_copies[i].wait()
                if i < 4:
                    w_copies[i + 4].start()
            both = dot_nt(w[b * 288 : b * 288 + 576], norm_out).astype(bf16)
        if b == 4:
            d_copies = fetch(
                [(d_refs[i], decoder.at[pl.ds(i * 256, 256)]) for i in range(4)], sems.at[2]
            )
            p_copies = fetch(
                [
                    (proj_ref.at[(x * 2 + z_at) * 2 + c], proj.at[pl.ds(i * 96, 96)])
                    for i, (x, c) in enumerate(places)
                ],
                sems.at[3],
            )
        at = b % 2 * 288
        q, k, v = [both[at + i * 96 : at + i * 96 + 96] for i in range(3)]
        keys = k.astype(f32).T.astype(bf16)
        values = v.astype(f32).T.astype(bf16)
        a = jnp.where(same, jnp.exp(dot(keys, q) * SCALE), 0.0)
        heads.append((q, k, values, a / jnp.sum(a, axis=0, keepdims=True)))
    first[1].wait()
    rows = [[], []]
    for x_from, c_from in [(x_at ^ k, c) for c in (core, 1 - core) for k in range(4)]:
        near = got[(x_from * 2 + z_at) * 2 + c_from].astype(f32)
        far = got[(x_from * 2 + 1 - z_at) * 2 + c_from].astype(f32)
        for r in range(2):
            lanes = slice(r * 64, r * 64 + 64)
            rows[r].append(jnp.concatenate([near[:, lanes], far[:, lanes]], axis=1))
    cells = jnp.concatenate([jnp.concatenate(row, axis=1) for row in rows], axis=0).astype(bf16)
    for copy in d_copies:
        copy.wait()
    token_grad = dot(cells, decoder[...])
    for copy in p_copies:
        copy.wait()
    grad_out = dot_nt(proj[...], token_grad.astype(bf16)).astype(bf16)
    stacked = []
    for b in range(8):
        q, k, values, a = heads[b]
        g = grad_out[b * 96 : b * 96 + 96]
        grad_v = dot_nt(g, a.astype(bf16))
        grad_a = dot(values, g)
        grad_s = a * (grad_a - jnp.sum(a * grad_a, axis=0, keepdims=True))
        grad_s = (grad_s * SCALE).astype(bf16)
        stacked += [dot(k, grad_s), dot_nt(q, grad_s), grad_v]
    stacked = jnp.concatenate(stacked, axis=0).T.astype(bf16)
    scaled = dot(stacked, w[...]) * gain
    mean = jnp.mean(scaled, axis=1, keepdims=True)
    slope = jnp.mean(scaled * normed, axis=1, keepdims=True)
    keep = jnp.where(z_at == 0, 1.0, 0.0)
    out = inv * (scaled - mean - normed * slope) + keep * token_grad
    out = out.T
    packed = []
    for g in range(16):
        tail = out[g * 96 + 72 : g * 96 + 96]
        for part in range(3):
            body = out[g * 96 + part * 24 : g * 96 + part * 24 + 24]
            packed.append(jnp.concatenate([body, tail[:, part * 32 : part * 32 + 32]], axis=1))
    out_ref[...] = jnp.concatenate(packed, axis=0).astype(bf16)


def final_kernel(shift_ref, part_ref, out_ref):
    shift = shift_ref[0]
    column = lax.broadcasted_iota(jnp.int32, (96, PAD), 1)
    parts = part_ref[...].astype(f32)
    sums = []
    for x in range(4):
        for c in range(2):
            at = (x * 4 + c) * 72
            s = parts[at : at + 72] + parts[at + 144 : at + 216]
            tail = jnp.concatenate([s[i * 24 : i * 24 + 24, 96:] for i in range(3)], axis=1)
            sums.append(jnp.concatenate([s[:, :96], tail], axis=0))
    for r in range(2):
        y = jnp.concatenate([s[:, r * GROUP : r * GROUP + GROUP] for s in sums], axis=1)
        y = jnp.where(column < shift, pltpu.roll(y, shift + PAD - COLS, 1), pltpu.roll(y, shift, 1))
        out_ref[r] = y[:, :COLS].astype(bf16)


VMEM = pl.BlockSpec(memory_space=pltpu.VMEM)
SMEM = pl.BlockSpec(memory_space=pltpu.SMEM)
HBM = pl.BlockSpec(memory_space=pltpu.HBM)


def call(kernel, outs, scalars, near, far=(), scratch=(), mib=16, flops=0, name=None, spaces=VMEM):
    arrays = [*near, *far]
    moved = sum(a.size * a.dtype.itemsize for a in arrays)
    moved += sum(math.prod(o.shape) * o.dtype.itemsize for o in jax.tree.leaves(outs))
    if isinstance(outs, list) and not isinstance(spaces, list):
        spaces = [spaces] * len(outs)
    return pl.pallas_call(
        kernel,
        out_shape=outs,
        in_specs=[SMEM] * len(scalars) + [VMEM] * len(near) + [HBM] * len(far),
        out_specs=spaces,
        scratch_shapes=scratch,
        compiler_params=pltpu.CompilerParams(vmem_limit_bytes=mib * MIB),
        cost_estimate=pl.CostEstimate(flops=flops, bytes_accessed=moved, transcendentals=0),
        name=name,
    )(*scalars, *arrays)


def shape(dims, kind=f32):
    return jax.ShapeDtypeStruct(dims, kind)


def body(tokens, shift, w_qkv, w_proj, ln_gain, w_dec, prediction, target, legendre):
    forward, back, cells = fourier_tables()
    place = lax.axis_index("loss")
    x_at, z_at, core = place // 2, place % 2, lax.axis_index("vars")
    group = ("loss", "vars")
    offset = shift[0]

    def along_x(block, step):
        pairs = [(x * 2 + z, (x + step) % 4 * 2 + z) for x in range(4) for z in range(2)]
        return lax.ppermute(block, "loss", pairs)

    def along_z(block):
        return lax.ppermute(block, "loss", [(i, i ^ 1) for i in range(8)])

    def across(block):
        return lax.ppermute(block, "vars", [(0, 1), (1, 0)])

    def after(block, earlier):
        return lax.optimization_barrier((block, earlier))[0]

    w_own = jnp.transpose(w_qkv, (1, 2, 3, 0)).reshape(3 * HEAD, D)
    w_all = [w_own, along_x(w_own, 1), along_x(w_own, 3), along_x(w_own, 2)]
    spectra = call(
        fourier_kernel,
        shape((256, 128)),
        [],
        [],
        [prediction.reshape(32, LON), target.reshape(32, LON), forward],
        scratch=[
            pltpu.VMEM((32, LON), bf16),
            pltpu.VMEM((32, LON), f32),
            pltpu.VMEM((LON, 512), bf16),
            pltpu.SemaphoreType.DMA((3,)),
        ],
        mib=60,
        flops=2 * 160 * LON * 512,
        name="fourier",
    )
    at_owners = lax.all_to_all(spectra.reshape(16, 16, 128), "proc", 0, 0, tiled=True)
    leg = call(
        cast_kernel,
        shape((16, LAT, LDEG), bf16),
        [],
        [after(legendre, spectra)],
        flops=BUSY,
        name="cast",
    )
    d_own = jnp.transpose(w_dec, (2, 0, 1, 3)).reshape(64, D)
    d_far = along_z(after(d_own, leg))
    powers = call(
        legendre_kernel,
        shape((16, 8, 640)),
        [],
        [at_owners, leg],
        scratch=[pltpu.VMEM((128, 128), f32)],
        flops=2 * 48 * 16 * LAT * LDEG,
        name="legendre",
    )
    d_own = call(
        pair_kernel,
        shape((128, D), bf16),
        [],
        [*after((d_own, d_far), (powers, w_all[1:3]))],
        flops=BUSY,
        name="pair",
    )
    d_far = lax.ppermute(d_own, "loss", [(i, i ^ 2) for i in range(8)])
    w_all += [across(after(w, d_own)) for w in w_all[:3]]
    powers = lax.all_to_all(powers, "proc", 0, 0, tiled=True)
    amse, grad_spectra = call(
        grad_kernel,
        [shape((8, 128)), shape((128, 128))],
        [],
        [after(powers, (d_own, w_all[1:3])), at_owners, leg],
        scratch=[
            pltpu.VMEM((128, 128), f32),
            pltpu.VMEM((128, 128), f32),
            pltpu.VMEM((8, 128), f32),
            pltpu.SemaphoreType.DMA,
        ],
        flops=2 * 80 * 16 * LAT * LDEG,
        name="grad",
        spaces=[HBM, VMEM],
    )
    banded = lax.all_to_all(grad_spectra.reshape(16, 8, 128), "proc", 0, 0, tiled=True)
    start = ((x_at * 2 + core) * GROUP + offset) % COLS
    back, cells = call(
        table_kernel,
        [shape((512, LON), bf16), shape((512, 4 * PAD), bf16)],
        [],
        [],
        [after(grad_spectra, w_all[1:3]), back, cells],
        scratch=[pltpu.SemaphoreType.DMA((2,))],
        flops=BUSY,
        name="tables",
    )
    d_own = call(
        pair_kernel,
        shape((256, D), bf16),
        [],
        [*after((d_own, d_far), grad_spectra)],
        flops=BUSY,
        name="pair2",
    )
    d_far = along_x(d_own, 2)
    d_all = [d_own, d_far, across(after(d_own, (back, w_all[4])))]
    field_grad, cell_grads = call(
        field_kernel,
        [shape((32, LON)), shape((16, GROUP, 128), bf16)],
        [shift],
        [banded, back, cells],
        scratch=[
            pltpu.VMEM((32, LON), f32),
            pltpu.VMEM((32, 512), f32),
            pltpu.SemaphoreType.DMA,
        ],
        flops=2 * 160 * LON * 512,
        name="field",
        spaces=[HBM, VMEM],
    )
    w_all.append(across(after(w_all[3], cell_grads)))
    own_tokens = after(tokens, cell_grads)
    own_tokens = jnp.concatenate([own_tokens, own_tokens[:, :GROUP]], axis=1)
    own_tokens = lax.dynamic_slice_in_dim(own_tokens, start, GROUP, 1).reshape(TOK, D)
    cell_grads = lax.all_to_all(cell_grads, group, 0, 0, tiled=True)
    gain = ln_gain.reshape(1, D)
    d_all.append(across(after(d_far, (cell_grads, own_tokens, gain))))
    parts = call(
        attention_kernel,
        shape((16 * 72, 128), bf16),
        [],
        [gain],
        [cell_grads, own_tokens, w_proj, *w_all, *d_all],
        scratch=[
            pltpu.VMEM((16, GROUP, 128), bf16),
            pltpu.VMEM((TOK, D), bf16),
            pltpu.VMEM((1024, D), bf16),
            pltpu.VMEM((8 * HEAD, D), bf16),
            pltpu.VMEM((8 * 3 * HEAD, D), bf16),
            pltpu.SemaphoreType.DMA((4, 8)),
        ],
        mib=60,
        flops=2 * TOK * D * (16 * 3 * HEAD + 1024 + 768),
        name="attention",
    )
    parts = lax.all_to_all(parts.reshape(16, 72, 128), group, 0, 0, tiled=True)
    input_grad = call(
        final_kernel, shape((2, HEAD, COLS), bf16), [shift], [parts.reshape(16 * 72, 128)], name="final"
    )
    return (
        amse[:4, 0],
        field_grad.reshape(4, 8, LON),
        jnp.transpose(input_grad, (0, 2, 1)),
    )


def solution(mesh):
    return jax.shard_map(
        body,
        mesh=mesh,
        in_specs=(
            P("proc", None, None),
            P(),
            P(None, None, ("loss", "vars"), None),
            P(),
            P(),
            P(("loss", "vars"), None, None, None),
            P(("loss", "vars"), "proc", None),
            P(("loss", "vars"), "proc", None),
            P("proc", None, None),
        ),
        out_specs=(
            P(("loss", "vars")),
            P(("loss", "vars"), "proc", None),
            P("proc", None, ("loss", "vars")),
        ),
        check_vma=False,
    )
```

```python
import math

import jax
import jax.numpy as jnp
import ml_dtypes
import numpy as np
from jax import lax
from jax.experimental import pallas as pl
from jax.experimental.pallas import tpu as pltpu
from jax.sharding import PartitionSpec as P

HEAD = 96
VARS = 64
LAT = 128
LON = 1440
LDEG = 384
MODES = 256
D = 1536
COLS = 360
WC = 12
GROUP = 48
TOK = 2 * GROUP
PAD = 384
EPSILON = 1e-06
NORM_EPSILON = 1e-05
SCALE = HEAD ** (-0.5)
f32, bf16 = jnp.float32, jnp.bfloat16
MIB = 1 << 20
BUSY = 1 << 33


def fourier_tables():
    column, wavenumber = np.arange(LON), np.arange(MODES)
    phase = (column[:, None] * wavenumber[None, :] % LON) * (2.0 * math.pi / LON)
    basis = np.stack([np.cos(phase), -np.sin(phase)], -1) / math.sqrt(LON)
    forward = basis.reshape(LON, 2 * MODES)
    back = basis.reshape(LON, 16, 16, 2).transpose(1, 3, 2, 0).reshape(2 * MODES, LON)
    cells = np.zeros((2 * MODES, 4, PAD))
    cells[:, :, :COLS] = back.reshape(2 * MODES, COLS, 4).transpose(0, 2, 1)
    tables = forward, back, cells.reshape(2 * MODES, 4 * PAD)
    return [jnp.asarray(table.astype(ml_dtypes.bfloat16)) for table in tables]


def dot(a, b):
    return lax.dot_general(a, b, (((1,), (0,)), ((), ())), preferred_element_type=f32)


def dot_nt(a, b):
    return lax.dot_general(a, b, (((1,), (1,)), ((), ())), preferred_element_type=f32)


def halves(x):
    high = x.astype(bf16)
    return high, (x - high.astype(f32)).astype(bf16)


def row_mask(shape):
    return lax.broadcasted_iota(jnp.int32, shape, 0) < 4


def swap_rows(x):
    return pltpu.roll(x, 4, 0)


def fetch(pairs, sems):
    copies = [pltpu.make_async_copy(src, dst, sems.at[i]) for i, (src, dst) in enumerate(pairs)]
    for copy in copies:
        copy.start()
    return copies


def fourier_kernel(pred_ref, targ_ref, table_ref, out_ref, pred, targ, table, sems):
    copies = fetch([(table_ref, table), (targ_ref, targ), (pred_ref, pred)], sems)
    for copy in copies:
        copy.wait()
    t_high, t_low = halves(targ[...])
    y = dot(jnp.concatenate([pred[...], t_high, t_low], axis=0), table[...])
    y = jnp.concatenate([y[:32], y[32:64] + y[64:]], axis=0)
    for part in range(32):
        lanes = slice(part * 16, part * 16 + 16)
        out_ref[part * 8 : part * 8 + 8, :] = jnp.concatenate(
            [y[fv * 8 : fv * 8 + 8, lanes] for fv in range(8)], axis=1
        )


def cast_kernel(leg_ref, out_ref):
    for m in range(16):
        out_ref[m] = leg_ref[m].astype(bf16)


def harmonics(spec_ref, leg_ref, turned, m):
    half, m8 = divmod(m, 8)
    if m8 == 0:
        turned[...] = spec_ref[:, half * 8 : half * 8 + 8, :].reshape(128, 128).T
    rows = [turned[pl.ds(m8 * 2 + c, 8, stride=16), :] for c in range(2)]
    high, low = halves(jnp.concatenate(rows, axis=0))
    both = dot(jnp.concatenate([high, low], axis=0), leg_ref[m])
    both = both[:16] + both[16:]
    return both[:8], both[8:]


def legendre_kernel(spec_ref, leg_ref, power_ref, turned):
    power = jnp.zeros((8, LDEG), f32)
    cross = jnp.zeros((8, LDEG), f32)
    for m in range(16):
        h0, h1 = harmonics(spec_ref, leg_ref, turned, m)
        power = power + h0 * h0 + h1 * h1
        cross = cross + h0 * swap_rows(h0) + h1 * swap_rows(h1)
    first = jnp.where(row_mask((8, 128)), cross[:, :128], cross[:, 128:256])
    block = jnp.concatenate([power, first, cross[:, 256:]], axis=1)
    for q in range(16):
        power_ref[q] = block


def grad_kernel(power_ref, spec_ref, leg_ref, amse_ref, out_ref, turned, grads, loss, sem):
    total = jnp.sum(power_ref[...], axis=0)
    upper = row_mask((8, LDEG))
    own = total[:, :LDEG]
    other = swap_rows(own)
    pp = jnp.where(upper, own, other)
    pt = jnp.where(upper, other, own)
    first = total[:, LDEG : LDEG + 128]
    second = swap_rows(first)
    top = row_mask((8, 128))
    cross = jnp.concatenate(
        [jnp.where(top, first, second), jnp.where(top, second, first), total[:, LDEG + 128 :]], axis=1
    )
    amp_p = jnp.sqrt(pp + EPSILON)
    amp_t = jnp.sqrt(pt + EPSILON)
    largest = jnp.maximum(pp, pt)
    incoherence = 1.0 - cross / (amp_p * amp_t)
    terms = (amp_p - amp_t) ** 2 + 2.0 * largest * incoherence
    amse = jnp.sum(terms, axis=1, keepdims=True) * (1.0 / (LDEG * MODES))
    loss[...] = jnp.broadcast_to(amse, (8, 128))
    copy = pltpu.make_async_copy(loss, amse_ref, sem)
    copy.start()
    share = jnp.where(pp > pt, 1.0, jnp.where(pp == pt, 0.5, 0.0))
    grad_p = (
        (amp_p - amp_t) / amp_p
        + 2.0 * share * incoherence
        + largest * cross / (amp_p * amp_p * amp_p * amp_t)
    )
    grad_c = -2.0 * largest / (amp_p * amp_t)
    weight = LAT * LON / (VARS * LDEG * MODES)
    factor = jnp.where(upper, 2.0 * grad_p, grad_c) * weight
    for m in range(16):
        h0, h1 = harmonics(spec_ref, leg_ref, turned, m)
        t0, t1 = factor * h0, factor * h1
        g = jnp.where(upper, t0 + swap_rows(t0), t1 + swap_rows(t1))
        high = g.astype(bf16).astype(f32)
        s = dot_nt(jnp.concatenate([high, g - high], axis=0).astype(bf16), leg_ref[m])
        grads[m * 8 : m * 8 + 8, :] = s[:8] + s[8:]
    sorted_rows = jnp.concatenate(
        [grads[pl.ds(c * 4 + v, 16, stride=8), :] for v in range(4) for c in range(2)], axis=0
    )
    out_ref[...] = sorted_rows.T
    copy.wait()


def pair_kernel(own_ref, far_ref, out_ref):
    size = own_ref.shape[0]
    out_ref[:size] = own_ref[...]
    out_ref[size:] = far_ref[...]


def table_kernel(tick_ref, table_ref, cell_ref, table, cell, sems):
    for copy in fetch([(cell_ref, cell), (table_ref, table)], sems):
        copy.wait()


def field_kernel(shift_ref, band_ref, table, cell, field_ref, out_ref, field, sorted_rows, sem):
    tiles = []
    for v in range(4):
        lanes = slice(v * 32, v * 32 + 32)
        tiles.append(jnp.concatenate([band_ref[q, :, lanes] for q in range(16)], axis=1))
    for v in range(4):
        sorted_rows[v * 4 : v * 4 + 4, :] = tiles[v][:4]
        sorted_rows[16 + v * 4 : 20 + v * 4, :] = tiles[v][4:]
    b_high, b_low = halves(jnp.concatenate(tiles, axis=0))
    a = dot(jnp.concatenate([b_high, b_low], axis=0), table[...])
    field[...] = a[:32] + a[32:]
    store = pltpu.make_async_copy(field, field_ref, sem)
    store.start()
    s_high, s_low = halves(sorted_rows[...])
    g = dot(jnp.concatenate([s_high, s_low], axis=0), cell[...])
    g = g[:32] + g[32:]
    g = jnp.concatenate(
        [g[r * 16 : r * 16 + 16, o * PAD : o * PAD + PAD] for r in range(2) for o in range(4)], axis=0
    )
    shift = shift_ref[0]
    column = lax.broadcasted_iota(jnp.int32, (128, PAD), 1)
    g = jnp.where(
        column < COLS - shift, pltpu.roll(g, PAD - shift, 1), pltpu.roll(g, COLS - shift, 1)
    )
    g = g.T.astype(bf16)
    for x in range(4):
        for z in range(2):
            for c in range(2):
                at = (x * 2 + c) * GROUP
                out_ref[x * 4 + z * 2 + c] = g[at : at + GROUP]
    store.wait()


def norm_rows(tok_ref, gain_ref):
    x = tok_ref[...].astype(f32)
    centred = x - jnp.mean(x, axis=1, keepdims=True)
    inv = lax.rsqrt(jnp.mean(centred * centred, axis=1, keepdims=True) + NORM_EPSILON)
    return centred * inv, inv


def attention_kernel(gain_ref, cells_ref, tok_ref, proj_ref, *refs):
    w_refs, d_refs, out_ref = refs[:8], refs[8:16], refs[16]
    got, tok, decoder, proj, w, sems = refs[17:]
    place, core = lax.axis_index("loss"), lax.axis_index("vars")
    x_at, z_at = place // 2, place % 2
    places = [((x_at + dx) % 4, c) for c in (core, 1 - core) for dx in (0, 3, 1, 2)]
    first = fetch([(tok_ref, tok), (cells_ref, got)], sems.at[0])
    w_copies = [
        pltpu.make_async_copy(w_refs[b], w.at[pl.ds(b * 288, 288)], sems.at[1, b]) for b in range(8)
    ]
    for copy in w_copies[:4]:
        copy.start()
    gain = gain_ref[...]
    row_window = lax.broadcasted_iota(jnp.int32, (TOK, TOK), 0) // WC
    col_window = lax.broadcasted_iota(jnp.int32, (TOK, TOK), 1) // WC
    same = row_window % 4 == col_window % 4
    first[0].wait()
    x = tok[...].astype(f32)
    centred = x - jnp.mean(x, axis=1, keepdims=True)
    inv = lax.rsqrt(jnp.mean(centred * centred, axis=1, keepdims=True) + NORM_EPSILON)
    normed = centred * inv
    norm_out = (normed * gain).astype(bf16)
    heads = []
    for b in range(8):
        if b % 2 == 0:
            for i in (b, b + 1):
                w_copies[i].wait()
                if i < 4:
                    w_copies[i + 4].start()
            both = dot_nt(w[b * 288 : b * 288 + 576], norm_out).astype(bf16)
        if b == 4:
            d_copies = fetch(
                [(d_refs[i], decoder.at[pl.ds(i * 128, 128)]) for i in range(8)], sems.at[2]
            )
            p_copies = fetch(
                [
                    (proj_ref.at[(x * 2 + z_at) * 2 + c], proj.at[pl.ds(i * 96, 96)])
                    for i, (x, c) in enumerate(places)
                ],
                sems.at[3],
            )
        at = b % 2 * 288
        q, k, v = [both[at + i * 96 : at + i * 96 + 96] for i in range(3)]
        keys = k.astype(f32).T.astype(bf16)
        values = v.astype(f32).T.astype(bf16)
        a = jnp.where(same, jnp.exp(dot(keys, q) * SCALE), 0.0)
        heads.append((q, k, values, a / jnp.sum(a, axis=0, keepdims=True)))
    first[1].wait()
    rows = [[], []]
    for x_from, c_from in places:
        near = got[(x_from * 2 + z_at) * 2 + c_from].astype(f32)
        far = got[(x_from * 2 + 1 - z_at) * 2 + c_from].astype(f32)
        for r in range(2):
            lanes = slice(r * 64, r * 64 + 64)
            rows[r].append(jnp.concatenate([near[:, lanes], far[:, lanes]], axis=1))
    cells = jnp.concatenate([jnp.concatenate(row, axis=1) for row in rows], axis=0).astype(bf16)
    for copy in d_copies:
        copy.wait()
    token_grad = dot(cells, decoder[...])
    for copy in p_copies:
        copy.wait()
    grad_out = dot_nt(proj[...], token_grad.astype(bf16)).astype(bf16)
    stacked = []
    for b in range(8):
        q, k, values, a = heads[b]
        g = grad_out[b * 96 : b * 96 + 96]
        grad_v = dot_nt(g, a.astype(bf16))
        grad_a = dot(values, g)
        grad_s = a * (grad_a - jnp.sum(a * grad_a, axis=0, keepdims=True))
        grad_s = (grad_s * SCALE).astype(bf16)
        stacked += [dot(k, grad_s), dot_nt(q, grad_s), grad_v]
    stacked = jnp.concatenate(stacked, axis=0).T.astype(bf16)
    scaled = dot(stacked, w[...]) * gain
    mean = jnp.mean(scaled, axis=1, keepdims=True)
    slope = jnp.mean(scaled * normed, axis=1, keepdims=True)
    keep = jnp.where(z_at == 0, 1.0, 0.0)
    out = inv * (scaled - mean - normed * slope) + keep * token_grad
    out = out.T
    packed = []
    for g in range(16):
        tail = out[g * 96 + 72 : g * 96 + 96]
        for part in range(3):
            body = out[g * 96 + part * 24 : g * 96 + part * 24 + 24]
            packed.append(jnp.concatenate([body, tail[:, part * 32 : part * 32 + 32]], axis=1))
    out_ref[...] = jnp.concatenate(packed, axis=0).astype(bf16)


def final_kernel(shift_ref, part_ref, out_ref):
    shift = shift_ref[0]
    column = lax.broadcasted_iota(jnp.int32, (96, PAD), 1)
    parts = part_ref[...].astype(f32)
    sums = []
    for x in range(4):
        for c in range(2):
            at = (x * 4 + c) * 72
            s = parts[at : at + 72] + parts[at + 144 : at + 216]
            tail = jnp.concatenate([s[i * 24 : i * 24 + 24, 96:] for i in range(3)], axis=1)
            sums.append(jnp.concatenate([s[:, :96], tail], axis=0))
    for r in range(2):
        y = jnp.concatenate([s[:, r * GROUP : r * GROUP + GROUP] for s in sums], axis=1)
        y = jnp.where(column < shift, pltpu.roll(y, shift + PAD - COLS, 1), pltpu.roll(y, shift, 1))
        out_ref[r] = y[:, :COLS].astype(bf16)


VMEM = pl.BlockSpec(memory_space=pltpu.VMEM)
SMEM = pl.BlockSpec(memory_space=pltpu.SMEM)
HBM = pl.BlockSpec(memory_space=pltpu.HBM)


def call(kernel, outs, scalars, near, far=(), scratch=(), mib=16, flops=0, name=None, spaces=VMEM):
    arrays = [*near, *far]
    moved = sum(a.size * a.dtype.itemsize for a in arrays)
    moved += sum(math.prod(o.shape) * o.dtype.itemsize for o in jax.tree.leaves(outs))
    if isinstance(outs, list) and not isinstance(spaces, list):
        spaces = [spaces] * len(outs)
    return pl.pallas_call(
        kernel,
        out_shape=outs,
        in_specs=[SMEM] * len(scalars) + [VMEM] * len(near) + [HBM] * len(far),
        out_specs=spaces,
        scratch_shapes=scratch,
        compiler_params=pltpu.CompilerParams(vmem_limit_bytes=mib * MIB),
        cost_estimate=pl.CostEstimate(flops=flops, bytes_accessed=moved, transcendentals=0),
        name=name,
    )(*scalars, *arrays)


def shape(dims, kind=f32):
    return jax.ShapeDtypeStruct(dims, kind)


def body(tokens, shift, w_qkv, w_proj, ln_gain, w_dec, prediction, target, legendre):
    forward, back, cells = fourier_tables()
    place = lax.axis_index("loss")
    x_at, z_at, core = place // 2, place % 2, lax.axis_index("vars")
    group = ("loss", "vars")
    offset = shift[0]

    def along_x(block, step):
        pairs = [(x * 2 + z, (x + step) % 4 * 2 + z) for x in range(4) for z in range(2)]
        return lax.ppermute(block, "loss", pairs)

    def along_z(block):
        return lax.ppermute(block, "loss", [(i, i ^ 1) for i in range(8)])

    def across(block):
        return lax.ppermute(block, "vars", [(0, 1), (1, 0)])

    def after(block, earlier):
        return lax.optimization_barrier((block, earlier))[0]

    w_own = jnp.transpose(w_qkv, (1, 2, 3, 0)).reshape(3 * HEAD, D)
    w_all = [w_own, along_x(w_own, 1), along_x(w_own, 3), along_x(w_own, 2)]
    spectra = call(
        fourier_kernel,
        shape((256, 128)),
        [],
        [],
        [prediction.reshape(32, LON), target.reshape(32, LON), forward],
        scratch=[
            pltpu.VMEM((32, LON), bf16),
            pltpu.VMEM((32, LON), f32),
            pltpu.VMEM((LON, 512), bf16),
            pltpu.SemaphoreType.DMA((3,)),
        ],
        mib=60,
        flops=2 * 160 * LON * 512,
        name="fourier",
    )
    at_owners = lax.all_to_all(spectra.reshape(16, 16, 128), "proc", 0, 0, tiled=True)
    leg = call(
        cast_kernel,
        shape((16, LAT, LDEG), bf16),
        [],
        [after(legendre, spectra)],
        flops=BUSY,
        name="cast",
    )
    d_own = jnp.transpose(w_dec, (2, 0, 1, 3)).reshape(64, D)
    d_far = along_z(after(d_own, leg))
    powers = call(
        legendre_kernel,
        shape((16, 8, 640)),
        [],
        [at_owners, leg],
        scratch=[pltpu.VMEM((128, 128), f32)],
        flops=2 * 48 * 16 * LAT * LDEG,
        name="legendre",
    )
    d_own = call(
        pair_kernel,
        shape((128, D), bf16),
        [],
        [*after((d_own, d_far), (powers, w_all[1:3]))],
        flops=BUSY,
        name="pair",
    )
    d_all = [d_own, along_x(d_own, 1), along_x(d_own, 3), along_x(d_own, 2)]
    w_all += [across(after(w, d_own)) for w in w_all[:3]]
    powers = lax.all_to_all(powers, "proc", 0, 0, tiled=True)
    amse, grad_spectra = call(
        grad_kernel,
        [shape((8, 128)), shape((128, 128))],
        [],
        [after(powers, (d_own, w_all[1:3])), at_owners, leg],
        scratch=[
            pltpu.VMEM((128, 128), f32),
            pltpu.VMEM((128, 128), f32),
            pltpu.VMEM((8, 128), f32),
            pltpu.SemaphoreType.DMA,
        ],
        flops=2 * 80 * 16 * LAT * LDEG,
        name="grad",
        spaces=[HBM, VMEM],
    )
    banded = lax.all_to_all(grad_spectra.reshape(16, 8, 128), "proc", 0, 0, tiled=True)
    start = ((x_at * 2 + core) * GROUP + offset) % COLS
    back, cells = call(
        table_kernel,
        [shape((512, LON), bf16), shape((512, 4 * PAD), bf16)],
        [],
        [],
        [after(grad_spectra, d_all[1:3]), back, cells],
        scratch=[pltpu.SemaphoreType.DMA((2,))],
        flops=BUSY,
        name="tables",
    )
    d_all.append(across(after(d_own, (back, w_all[4]))))
    d_all += [across(after(d, back)) for d in d_all[1:3]]
    field_grad, cell_grads = call(
        field_kernel,
        [shape((32, LON)), shape((16, GROUP, 128), bf16)],
        [shift],
        [banded, back, cells],
        scratch=[
            pltpu.VMEM((32, LON), f32),
            pltpu.VMEM((32, 512), f32),
            pltpu.SemaphoreType.DMA,
        ],
        flops=2 * 160 * LON * 512,
        name="field",
        spaces=[HBM, VMEM],
    )
    own_tokens = after(tokens, cell_grads)
    own_tokens = jnp.concatenate([own_tokens, own_tokens[:, :GROUP]], axis=1)
    own_tokens = lax.dynamic_slice_in_dim(own_tokens, start, GROUP, 1).reshape(TOK, D)
    cell_grads = lax.all_to_all(cell_grads, group, 0, 0, tiled=True)
    gain = ln_gain.reshape(1, D)
    w_all.append(across(after(w_all[3], (cell_grads, own_tokens, gain))))
    d_all.append(across(after(d_all[3], (cell_grads, own_tokens, gain))))
    parts = call(
        attention_kernel,
        shape((16 * 72, 128), bf16),
        [],
        [gain],
        [cell_grads, own_tokens, w_proj, *w_all, *d_all],
        scratch=[
            pltpu.VMEM((16, GROUP, 128), bf16),
            pltpu.VMEM((TOK, D), bf16),
            pltpu.VMEM((1024, D), bf16),
            pltpu.VMEM((8 * HEAD, D), bf16),
            pltpu.VMEM((8 * 3 * HEAD, D), bf16),
            pltpu.SemaphoreType.DMA((4, 8)),
        ],
        mib=60,
        flops=2 * TOK * D * (16 * 3 * HEAD + 1024 + 768),
        name="attention",
    )
    parts = lax.all_to_all(parts.reshape(16, 72, 128), group, 0, 0, tiled=True)
    input_grad = call(
        final_kernel, shape((2, HEAD, COLS), bf16), [shift], [parts.reshape(16 * 72, 128)], name="final"
    )
    return (
        amse[:4, 0],
        field_grad.reshape(4, 8, LON),
        jnp.transpose(input_grad, (0, 2, 1)),
    )


def solution(mesh):
    return jax.shard_map(
        body,
        mesh=mesh,
        in_specs=(
            P("proc", None, None),
            P(),
            P(None, None, ("loss", "vars"), None),
            P(),
            P(),
            P(("loss", "vars"), None, None, None),
            P(("loss", "vars"), "proc", None),
            P(("loss", "vars"), "proc", None),
            P("proc", None, None),
        ),
        out_specs=(
            P(("loss", "vars")),
            P(("loss", "vars"), "proc", None),
            P("proc", None, ("loss", "vars")),
        ),
        check_vma=False,
    )
```
